256 devices in a mesh: row: 8 (over z_hi, core), col: 32 (over z_lo, x, y).
Axes of the slice: x: 4, y: 4, z: 8 (z_hi: 4, z_lo: 2; z = z_hi * 2 + z_lo), core: 2. Of those that a mesh axis runs over, the one named last changes fastest.
Arguments:
- amplitudes: float32 [512, 32768], P('row', 'col'), may hold values from -6 to 6
- integrals: float32 [256, 8, 128, 128], P('col'), may hold values from -0.1875 to 0.1875
- sources: int32 [256, 8], P('col'), may hold values from 0 to 255, as said below
- counts: int32 [256], P('col'), may hold values from 4 to 8, as said below
- tile_irrep: int32 [256], replicated, may hold values from 0 to 7, as said below
- partner: int32 [256], replicated, may hold values from 0 to 255, as said below
- occ_energy: float32 [512], P('row'), may hold values from -3 to -1
- virt_energy: float32 [32768], P('col'), may hold values from 1 to 5
Outputs:
- update: float32 [512, 32768], P('row', 'col')
The draws below stay inside these ranges and needn't reach their ends.
Inputs may be any that keep to these rules, and one draw needn't show every extreme that they name: `sources`: each row lists 8 different tiles; in some rows one of them has another representation than the output tile, the others share it. `counts`: some tile has 8 counted sources. `tile_irrep`: each of the 8 representations labels exactly 32 tiles. An involution without fixed points that keeps the representation; partner[p] // 8 and p // 8 differ by 16.
All inputs are finite; a program needn't handle non-finite values.
Results may differ from the reference program's by a relative error of at most 0.0003.
Values sent between devices are 32-bit elements; how exact they have to be, the bound alone decides.
No kernel may reach another device: no remote copies, remote signals or barrier semaphores. Data moves between devices by JAX's collectives and lax.ppermute only.
A program may use at most 64 MiB of HBM per device.

```python
import jax
import jax.numpy as jnp
from jax import lax

TILE = 128
KMAX = 8
TPD = 8
NT = 256
OP = 512


def tile_layout(key):
    groups = NT // TPD
    half_groups = groups // 2
    half_tiles = NT // 2
    first_key = jax.random.fold_in(key, 11)
    second_key = jax.random.fold_in(key, 12)
    base = jax.random.permutation(first_key, half_tiles).astype(jnp.int32)
    irrep_first = (jnp.arange(half_tiles, dtype=jnp.int32) % 8)[base]
    perm_keys = jax.random.split(second_key, half_groups)
    perms = jax.vmap(lambda kk: jax.random.permutation(kk, TPD))(perm_keys).astype(jnp.int32)
    first_idx = jnp.arange(half_tiles, dtype=jnp.int32)
    group = first_idx // TPD
    slot = first_idx % TPD
    mate = (group + half_groups) * TPD + perms[group, slot]
    partner = jnp.zeros((NT,), jnp.int32).at[first_idx].set(mate).at[mate].set(first_idx)
    irrep = jnp.zeros((NT,), jnp.int32).at[first_idx].set(irrep_first).at[mate].set(irrep_first)
    return (irrep, partner)


def draw_tile_irrep(key, part):
    irrep, partner = tile_layout(key)
    return irrep.astype(jnp.int32)


def draw_partner(key, part):
    irrep, partner = tile_layout(key)
    return partner.astype(jnp.int32)


def draw_sources(key, part):
    irrep, partner = tile_layout(key)
    key = jax.random.fold_in(key, 5)
    keys = jax.random.split(key, 6)
    rank = jax.random.permutation(keys[0], NT).astype(jnp.int32)
    order = jnp.argsort(irrep * NT + rank).astype(jnp.int32)
    class_size = NT // 8
    offset = jax.random.randint(keys[1], (NT,), 0, class_size)
    spots = (offset[:, None] + jnp.arange(KMAX, dtype=jnp.int32)[None, :]) % class_size
    members = order[irrep[:, None] * class_size + spots]
    other_class = (irrep + jax.random.randint(keys[2], (NT,), 1, 8)) % 8
    other_spot = jax.random.randint(keys[3], (NT,), 0, class_size)
    stranger = order[other_class * class_size + other_spot]
    place = jax.random.randint(keys[4], (NT,), 0, KMAX)
    flip = jax.random.randint(keys[5], (NT,), 0, 2) == 1
    hit = (jnp.arange(KMAX, dtype=jnp.int32)[None, :] == place[:, None]) & flip[:, None]
    return jnp.where(hit, stranger[:, None], members).astype(jnp.int32)


def draw_counts(key, part):
    key = jax.random.fold_in(key, 7)
    first, second = jax.random.split(key)
    values = jax.random.randint(first, (NT,), KMAX // 2, KMAX + 1)
    spot = jax.random.randint(second, (), 0, NT)
    return values.at[spot].set(KMAX).astype(jnp.int32)


def level_of(own_key, shape, pieces, smallest, top_value):
    def one(position, shards_of):
        heights = jax.random.uniform(jax.random.fold_in(jax.random.fold_in(own_key, 6), position), (shards_of,), jnp.float32, smallest / len(pieces), top_value / len(pieces))
        return jnp.repeat(jnp.exp(heights), shape[position] // shards_of).reshape((-1,) + (1,) * (len(shape) - position - 1))

    level = one(*pieces[0])
    for cut in pieces[1:]:
        level = level * one(*cut)
    return level


def scatter_about(rng, shape, scale, reach, pieces=(), kind=jnp.bfloat16):
    result = jax.random.normal(rng, shape, jnp.float32) * scale
    if len(pieces) > 0:
        result = level_of(rng, shape, pieces, -0.22, 0.18) * result
    return jnp.clip(result, min=-reach, max=reach).astype(kind)


def setup_inputs(seed: int = 0) -> dict:
    streams_of = jax.random.split(jax.random.key(seed), 9)
    return {
        "amplitudes": scatter_about(streams_of[0], (OP, NT * TILE), 1.0, 6.0, ((0, 8), (1, 32)), jnp.float32),
        "integrals": scatter_about(streams_of[1], (NT, KMAX, TILE, TILE), (KMAX * TILE) ** -0.5, 0.1875, ((0, 32),), jnp.float32),
        "sources": draw_sources(jax.random.fold_in(streams_of[8], 71), 0),
        "counts": draw_counts(jax.random.fold_in(streams_of[8], 71), 0),
        "tile_irrep": draw_tile_irrep(jax.random.fold_in(streams_of[8], 71), 0),
        "partner": draw_partner(jax.random.fold_in(streams_of[8], 71), 0),
        "occ_energy": jnp.clip(-3.0 + 2.0 * jax.random.uniform(streams_of[6], (OP,), jnp.float32) ** level_of(streams_of[6], (OP,), ((0, 8),), -0.2, 0.2), -3.0, -1.0),
        "virt_energy": jnp.clip(1.0 + 4.0 * jax.random.uniform(streams_of[7], (NT * TILE,), jnp.float32) ** level_of(streams_of[7], (NT * TILE,), ((0, 32),), -0.2, 0.2), 1.0, 5.0),
    }


def reference(amplitudes, integrals, sources, counts, tile_irrep, partner, occ_energy, virt_energy):
    whole = amplitudes.reshape(OP, NT, TILE)

    def one_tile(index):
        src = sources[index]
        live = (jnp.arange(KMAX, dtype=jnp.int32) < counts[index]) & (tile_irrep[src] == tile_irrep[index])
        picked = whole[:, src, :]
        picked = jnp.where(live[None, :, None], picked, jnp.float32(0.0))
        return jnp.einsum("okc,kce->oe", picked, integrals[index], precision=lax.Precision.HIGHEST)

    ladder = lax.map(one_tile, jnp.arange(NT, dtype=jnp.int32))
    ladder = jnp.transpose(ladder, (1, 0, 2))
    rolled = jnp.roll(ladder, OP // 2, axis=0)
    mirrored = rolled[:, partner, :]
    denom = occ_energy[:, None, None] - virt_energy.reshape(1, NT, TILE)
    update = (ladder + mirrored) / denom
    return update.reshape(OP, NT * TILE)
```

```python
import jax
import jax.numpy as jnp
from jax import lax
from jax.experimental import pallas as pl
from jax.experimental.pallas import tpu as pltpu
from jax.sharding import PartitionSpec as P

LANES = 128
SUB = 8
VMEM = pl.BlockSpec(memory_space=pltpu.VMEM)
SMEM = pl.BlockSpec(memory_space=pltpu.SMEM)


def halves(x):
    high = x.astype(jnp.bfloat16)
    low = (x - high.astype(jnp.float32)).astype(jnp.bfloat16)
    return high, low


def spread(groups, mine, depth, rows, tiles, src_ref, cnt_ref, irr_ref, amp_ref, out_ref):
    first = lax.axis_index("col") * mine
    share = rows // groups
    chunk = share * mine + SUB
    lane = lax.broadcasted_iota(jnp.int32, (SUB, LANES), 1)
    keys = jnp.full((SUB, LANES), -1, jnp.int32)
    for m in range(mine):
        base = irr_ref[first + m] * tiles
        count = cnt_ref[m]
        for k in range(depth):
            key = jnp.where(k < count, src_ref[m, k] + base, -1)
            keys = jnp.where(lane == m * depth + k, key, keys)
    keys = keys.astype(jnp.float32)
    for j in range(groups):
        out_ref[pl.ds(j * chunk + share * mine, SUB), :] = keys
    for i in range(rows // SUB):
        r, j = divmod(i * SUB, groups)
        for m in range(mine):
            out_ref[pl.ds(j * chunk + r * mine + m, SUB, stride=chunk), :] = amp_ref[
                pl.ds(i * SUB, SUB), pl.ds(m * LANES, LANES)
            ]


def pick(groups, mine, slots, share, tiles, irr_ref, got_ref, out_ref, hot_ref):
    chunk = share * mine + SUB
    table = jnp.concatenate(
        [
            jnp.concatenate(
                [got_ref[pl.ds(g * chunk + r * mine, mine), :] for g in range(groups)], axis=0
            )
            for r in range(share)
        ],
        axis=1,
    )
    high, low = halves(table)
    both = jnp.concatenate([high, low], axis=1)
    lists = got_ref[pl.ds(share * mine, groups, stride=chunk), :]
    lists = jnp.concatenate([lists, jnp.zeros((LANES - groups, LANES), jnp.float32)], axis=0)
    lists = lists.T
    tile = lax.broadcasted_iota(jnp.int32, (1, tiles), 1)
    label = (irr_ref[...] * tiles + tile).astype(jnp.float32)
    for g in range(groups):
        hot = lists[:slots, g : g + 1] == label
        hot_ref[pl.ds(g * slots, slots), :] = jnp.where(hot, 1.0, 0.0).astype(jnp.bfloat16)
    width = share * LANES
    step = 512
    for b in range(groups * slots // step):
        sums = jnp.dot(
            hot_ref[pl.ds(b * step, step), :], both, preferred_element_type=jnp.float32
        )
        sums = sums[:, :width] + sums[:, width:]
        for g in range(step // slots):
            for r in range(share):
                to = ((b * step // slots + g) * share + r) * slots
                out_ref[pl.ds(to, slots), :] = sums[
                    g * slots : (g + 1) * slots, r * LANES : (r + 1) * LANES
                ]


def multiply(groups, mine, depth, rows, got_ref, int_ref, out_ref):
    slots = mine * depth
    share = rows // groups
    for m in range(mine):
        cols = []
        for k in range(depth):
            cols.append(
                jnp.concatenate(
                    [
                        got_ref[pl.ds(r * slots + m * depth + k, groups, stride=share * slots), :]
                        for r in range(share)
                    ],
                    axis=0,
                )
            )
        left_high, left_low = halves(jnp.concatenate(cols, axis=1))
        right_high, right_low = halves(int_ref[pl.ds(m * depth * LANES, depth * LANES), :])
        sums = jnp.dot(
            jnp.concatenate([left_high, left_low], axis=0),
            jnp.concatenate([right_high, right_low], axis=1),
            preferred_element_type=jnp.float32,
        )
        sums = sums[:, :LANES] + sums[:, LANES:]
        out_ref[m] = sums[:rows] + sums[rows:]


def finish(mine, rows, half_col, cols, par_ref, lad_ref, mir_ref, occ_ref, virt_ref, out_ref):
    me = lax.axis_index("col")
    other_first = lax.rem(me + half_col, cols) * mine
    row = lax.broadcasted_iota(jnp.int32, (rows, rows), 0)
    col = lax.broadcasted_iota(jnp.int32, (rows, rows), 1)
    occ = jnp.sum(jnp.where(row == col, occ_ref[...], 0.0), axis=1, keepdims=True)
    for m in range(mine):
        at = par_ref[me * mine + m] - other_first
        lanes = pl.ds(m * LANES, LANES)
        out_ref[:, lanes] = (lad_ref[m] + mir_ref[at]) / (occ - virt_ref[:, lanes])


def shards(amplitudes, integrals, sources, counts, tile_irrep, partner, occ_energy, virt_energy):
    rows = amplitudes.shape[0]
    mine, depth, width, _ = integrals.shape
    tiles = tile_irrep.shape[0]
    cols = lax.axis_size("col")
    heights = lax.axis_size("row")
    slots = mine * depth
    share = rows // cols
    chunk = share * mine + SUB
    f32 = jnp.float32

    def call(body, out, *args, specs, scratch=(), flops=0, moved=0):
        return pl.pallas_call(
            body,
            out_shape=jax.ShapeDtypeStruct(out, f32),
            in_specs=specs,
            out_specs=VMEM,
            scratch_shapes=scratch,
            compiler_params=pltpu.CompilerParams(vmem_limit_bytes=40 * 1024 * 1024),
            cost_estimate=pl.CostEstimate(flops=flops, bytes_accessed=moved, transcendentals=0),
        )(*args)

    sent = call(
        lambda *refs: spread(cols, mine, depth, rows, tiles, *refs),
        (cols * chunk, LANES),
        sources, counts, tile_irrep, amplitudes,
        specs=[SMEM, SMEM, SMEM, VMEM],
        moved=2 * amplitudes.size * 4,
    )
    got = lax.all_to_all(sent.reshape(cols, chunk, LANES), "col", 0, 0)
    sent = call(
        lambda *refs: pick(cols, mine, slots, share, tiles, *refs),
        (cols * share * slots, LANES),
        tile_irrep.reshape(1, tiles), got.reshape(cols * chunk, LANES),
        specs=[VMEM, VMEM],
        scratch=[pltpu.VMEM((cols * slots, tiles), jnp.bfloat16)],
        flops=4 * cols * slots * tiles * share * LANES,
        moved=cols * slots * share * LANES * 4,
    )
    got = lax.all_to_all(sent.reshape(cols, share * slots, LANES), "col", 0, 0)
    ladder = call(
        lambda *refs: multiply(cols, mine, depth, rows, *refs),
        (mine, rows, width),
        got.reshape(cols * share * slots, LANES),
        integrals.reshape(mine * depth * width, width),
        specs=[VMEM, VMEM],
        flops=8 * rows * mine * depth * width * width,
        moved=integrals.size * 4 + got.size * 4,
    )
    pairs = [
        (r * cols + c, (r + heights // 2) % heights * cols + (c + cols // 2) % cols)
        for r in range(heights)
        for c in range(cols)
    ]
    mirrored = lax.ppermute(ladder, ("row", "col"), pairs)
    return call(
        lambda *refs: finish(mine, rows, cols // 2, cols, *refs),
        (rows, mine * width),
        partner, ladder, mirrored, occ_energy.reshape(1, rows), virt_energy.reshape(1, mine * width),
        specs=[SMEM, VMEM, VMEM, VMEM, VMEM],
        moved=4 * rows * mine * width * 3,
    )


def solution(mesh):
    placed = (
        P("row", "col"),
        P("col", None, None, None),
        P("col", None),
        P("col"),
        P(),
        P(),
        P("row"),
        P("col"),
    )
    return jax.shard_map(
        shards, mesh=mesh, in_specs=placed, out_specs=P("row", "col"), check_vma=False
    )
```

```python
import jax
import jax.numpy as jnp
from jax import lax
from jax.experimental import pallas as pl
from jax.experimental.pallas import tpu as pltpu
from jax.sharding import PartitionSpec as P

LANES = 128
SUB = 8
VMEM = pl.BlockSpec(memory_space=pltpu.VMEM)
HBM = pl.BlockSpec(memory_space=pltpu.HBM)


def halves(x):
    high = x.astype(jnp.bfloat16)
    low = (x - high.astype(jnp.float32)).astype(jnp.bfloat16)
    return high, low


def spread(
    groups, mine, depth, rows, tiles,
    src_hbm, cnt_hbm, irr_hbm, row_hbm, amp_hbm, out_ref,
    src_ref, cnt_ref, irr_ref, row_ref, amp_ref, sems,
):
    pairs = [
        (amp_hbm, amp_ref), (irr_hbm, irr_ref), (src_hbm, src_ref), (cnt_hbm, cnt_ref),
        (row_hbm, row_ref),
    ]
    copies = [pltpu.make_async_copy(a, b, sems.at[n]) for n, (a, b) in enumerate(pairs)]
    for copy in copies:
        copy.start()
    first = lax.axis_index("col") * mine
    share = rows // groups
    chunk = share * mine + SUB
    for copy in copies[1:]:
        copy.wait()
    lane = lax.broadcasted_iota(jnp.int32, (SUB, LANES), 1)
    keys = jnp.full((SUB, LANES), -1, jnp.int32)
    for m in range(mine):
        base = irr_ref[first + m] * tiles
        count = cnt_ref[m]
        for k in range(depth):
            key = jnp.where(k < count, src_ref[m, k] + base, -1)
            keys = jnp.where(lane == m * depth + k, key, keys)
    line = lax.broadcasted_iota(jnp.int32, (SUB, LANES), 0)
    for n in range(tiles // LANES):
        label = row_ref[:, pl.ds(n * LANES, LANES)] * tiles + n * LANES
        keys = jnp.where(line == n + 1, label + lane, keys)
    keys = keys.astype(jnp.float32)
    for j in range(groups):
        out_ref[pl.ds(j * chunk + share * mine, SUB), :] = keys
    copies[0].wait()
    for i in range(rows // SUB):
        r, j = divmod(i * SUB, groups)
        for m in range(mine):
            out_ref[pl.ds(j * chunk + r * mine + m, SUB, stride=chunk), :] = amp_ref[
                pl.ds(i * SUB, SUB), pl.ds(m * LANES, LANES)
            ]


def pick(groups, mine, slots, share, tiles, got_ref, out_ref, hot_ref):
    chunk = share * mine + SUB
    table = jnp.concatenate(
        [
            jnp.concatenate(
                [got_ref[pl.ds(g * chunk + r * mine, mine), :] for g in range(groups)], axis=0
            )
            for r in range(share)
        ],
        axis=1,
    )
    high, low = halves(table)
    both = jnp.concatenate([high, low], axis=1)
    lists = got_ref[pl.ds(share * mine, groups, stride=chunk), :]
    lists = jnp.concatenate([lists, jnp.zeros((LANES - groups, LANES), jnp.float32)], axis=0)
    lists = lists.T
    label = jnp.concatenate(
        [got_ref[pl.ds(share * mine + 1 + n, 1), :] for n in range(tiles // LANES)], axis=1
    )
    for g in range(groups):
        hot = lists[:slots, g : g + 1] == label
        hot_ref[pl.ds(g * slots, slots), :] = jnp.where(hot, 1.0, 0.0).astype(jnp.bfloat16)
    width = share * LANES
    step = 512
    for b in range(groups * slots // step):
        sums = jnp.dot(
            hot_ref[pl.ds(b * step, step), :], both, preferred_element_type=jnp.float32
        )
        sums = sums[:, :width] + sums[:, width:]
        for g in range(step // slots):
            for r in range(share):
                to = ((b * step // slots + g) * share + r) * slots
                out_ref[pl.ds(to, slots), :] = sums[
                    g * slots : (g + 1) * slots, r * LANES : (r + 1) * LANES
                ]


def multiply(
    groups, half, mine, depth, rows, par_hbm, got_ref, int_ref, out_ref, turned_ref, par_ref, sem
):
    copy = pltpu.make_async_copy(par_hbm, par_ref, sem)
    copy.start()
    slots = mine * depth
    share = rows // groups
    me = lax.axis_index("col")
    other_first = lax.rem(me + half, groups) * mine
    for m in range(mine):
        cols = []
        for k in range(depth):
            cols.append(
                jnp.concatenate(
                    [
                        got_ref[pl.ds(r * slots + m * depth + k, groups, stride=share * slots), :]
                        for r in range(share)
                    ],
                    axis=0,
                )
            )
        left_high, left_low = halves(jnp.concatenate(cols, axis=1))
        right_high, right_low = halves(int_ref[pl.ds(m * depth * LANES, depth * LANES), :])
        sums = jnp.dot(
            jnp.concatenate([left_high, left_low], axis=0),
            jnp.concatenate([right_high, right_low], axis=1),
            preferred_element_type=jnp.float32,
        )
        sums = sums[:, :LANES] + sums[:, LANES:]
        sums = sums[:rows] + sums[rows:]
        out_ref[m] = sums
        if m == 0:
            copy.wait()
        turned_ref[par_ref[me * mine + m] - other_first] = sums


def finish(mine, rows, lad_ref, mir_ref, occ_ref, virt_ref, out_ref):
    row = lax.broadcasted_iota(jnp.int32, (rows, rows), 0)
    col = lax.broadcasted_iota(jnp.int32, (rows, rows), 1)
    occ = jnp.sum(jnp.where(row == col, occ_ref[...], 0.0), axis=1, keepdims=True)
    for m in range(mine):
        lanes = pl.ds(m * LANES, LANES)
        out_ref[:, lanes] = (lad_ref[m] + mir_ref[m]) / (occ - virt_ref[:, lanes])


def shards(amplitudes, integrals, sources, counts, tile_irrep, partner, occ_energy, virt_energy):
    rows = amplitudes.shape[0]
    mine, depth, width, _ = integrals.shape
    tiles = tile_irrep.shape[0]
    cols = lax.axis_size("col")
    heights = lax.axis_size("row")
    slots = mine * depth
    share = rows // cols
    chunk = share * mine + SUB
    f32 = jnp.float32

    def call(body, out, *args, specs, scratch=(), flops=0, moved=0, room=40):
        return pl.pallas_call(
            body,
            out_shape=[jax.ShapeDtypeStruct(shape, f32) for shape in out],
            in_specs=specs,
            out_specs=[VMEM] * len(out),
            scratch_shapes=scratch,
            compiler_params=pltpu.CompilerParams(vmem_limit_bytes=room * 1024 * 1024),
            cost_estimate=pl.CostEstimate(flops=flops, bytes_accessed=moved, transcendentals=0),
        )(*args)

    (sent,) = call(
        lambda *refs: spread(cols, mine, depth, rows, tiles, *refs),
        [(cols * chunk, LANES)],
        sources, counts, tile_irrep, tile_irrep.reshape(1, tiles), amplitudes,
        specs=[HBM] * 5,
        scratch=[
            pltpu.SMEM(sources.shape, jnp.int32),
            pltpu.SMEM(counts.shape, jnp.int32),
            pltpu.SMEM((tiles,), jnp.int32),
            pltpu.VMEM((1, tiles), jnp.int32),
            pltpu.VMEM(amplitudes.shape, f32),
            pltpu.SemaphoreType.DMA((5,)),
        ],
        moved=2 * amplitudes.size * 4,
        room=63,
    )
    got = lax.all_to_all(sent.reshape(cols, chunk, LANES), "col", 0, 0)
    (sent,) = call(
        lambda *refs: pick(cols, mine, slots, share, tiles, *refs),
        [(cols * share * slots, LANES)],
        got.reshape(cols * chunk, LANES),
        specs=[VMEM],
        scratch=[pltpu.VMEM((cols * slots, tiles), jnp.bfloat16)],
        flops=4 * cols * slots * tiles * share * LANES,
        moved=cols * slots * share * LANES * 4,
    )
    got = lax.all_to_all(sent.reshape(cols, share * slots, LANES), "col", 0, 0)
    ladder, turned = call(
        lambda *refs: multiply(cols, cols // 2, mine, depth, rows, *refs),
        [(mine, rows, width)] * 2,
        partner,
        got.reshape(cols * share * slots, LANES),
        integrals.reshape(mine * depth * width, width),
        specs=[HBM, VMEM, VMEM],
        scratch=[pltpu.SMEM((tiles,), jnp.int32), pltpu.SemaphoreType.DMA],
        flops=8 * rows * mine * depth * width * width,
        moved=integrals.size * 4 + got.size * 4,
    )
    pairs = [
        (r * cols + c, (r + heights // 2) % heights * cols + (c + cols // 2) % cols)
        for r in range(heights)
        for c in range(cols)
    ]
    mirrored = lax.ppermute(turned, ("row", "col"), pairs)
    (update,) = call(
        lambda *refs: finish(mine, rows, *refs),
        [(rows, mine * width)],
        ladder, mirrored, occ_energy.reshape(1, rows), virt_energy.reshape(1, mine * width),
        specs=[VMEM] * 4,
        moved=4 * rows * mine * width * 3,
    )
    return update


def solution(mesh):
    placed = (
        P("row", "col"),
        P("col", None, None, None),
        P("col", None),
        P("col"),
        P(),
        P(),
        P("row"),
        P("col"),
    )
    return jax.shard_map(
        shards, mesh=mesh, in_specs=placed, out_specs=P("row", "col"), check_vma=False
    )
```

```python
import jax
import jax.numpy as jnp
from jax import lax
from jax.experimental import pallas as pl
from jax.experimental.pallas import tpu as pltpu
from jax.sharding import PartitionSpec as P

LANES = 128
SUB = 8
VMEM = pl.BlockSpec(memory_space=pltpu.VMEM)
HBM = pl.BlockSpec(memory_space=pltpu.HBM)
SMEM = pl.BlockSpec(memory_space=pltpu.SMEM)
USUAL = 52


def halves(x):
    high = x.astype(jnp.bfloat16)
    low = (x - high.astype(jnp.float32)).astype(jnp.bfloat16)
    return high, low


def spread(
    groups, mine, depth, rows, tiles,
    src_hbm, cnt_hbm, irr_hbm, row_hbm, amp_hbm, out_ref, place_ref,
    src_ref, cnt_ref, irr_ref, row_ref, amp_ref, sems,
):
    pairs = [
        (amp_hbm, amp_ref), (irr_hbm, irr_ref), (src_hbm, src_ref), (cnt_hbm, cnt_ref),
        (row_hbm, row_ref),
    ]
    copies = [pltpu.make_async_copy(a, b, sems.at[n]) for n, (a, b) in enumerate(pairs)]
    for copy in copies:
        copy.start()
    me = lax.axis_index("col")
    share = rows // groups
    chunk = share * mine + SUB
    before = lax.broadcasted_iota(jnp.int32, (tiles, tiles), 0)
    after = lax.broadcasted_iota(jnp.int32, (tiles, tiles), 1)
    earlier = jnp.where(before < after, 1.0, 0.0).astype(jnp.bfloat16)
    for copy in copies[1:]:
        copy.wait()
    tile = lax.broadcasted_iota(jnp.int32, (1, tiles), 1)
    label = row_ref[...] * tiles + tile
    listed = jnp.zeros((1, tiles), jnp.int32)
    for m in range(mine):
        base = irr_ref[me * mine + m] * tiles
        count = cnt_ref[m]
        for k in range(depth):
            key = jnp.where(k < count, src_ref[m, k] + base, -1)
            listed = jnp.where(label == key, 1, listed)
    owned = (tile >= me * mine) & (tile < me * mine + mine)
    listed = jnp.where(owned, 0, listed)
    rank = jnp.dot(
        jnp.broadcast_to(listed, (2 * SUB, tiles)).astype(jnp.float32).astype(jnp.bfloat16),
        earlier,
        preferred_element_type=jnp.float32,
    )[:1]
    place = jnp.where(listed > 0, rank, -1.0)
    place_ref[...] = place.astype(jnp.int32)
    line = lax.broadcasted_iota(jnp.int32, (SUB, LANES), 0)
    sheet = jnp.zeros((SUB, LANES), jnp.float32)
    for n in range(tiles // LANES):
        sheet = jnp.where(line == n, place[:, n * LANES : (n + 1) * LANES], sheet)
    for j in range(groups):
        out_ref[pl.ds(j * chunk + share * mine, SUB), :] = sheet
    copies[0].wait()
    for i in range(rows // SUB):
        r, j = divmod(i * SUB, groups)
        for m in range(mine):
            out_ref[pl.ds(j * chunk + r * mine + m, SUB, stride=chunk), :] = amp_ref[
                pl.ds(i * SUB, SUB), pl.ds(m * LANES, LANES)
            ]


def pick(groups, mine, slots, usual, share, tiles, got_ref, out_ref, rest_ref, more_ref, hot_ref):
    chunk = share * mine + SUB
    table = jnp.concatenate(
        [
            jnp.concatenate(
                [got_ref[pl.ds(g * chunk + r * mine, mine), :] for g in range(groups)], axis=0
            )
            for r in range(share)
        ],
        axis=1,
    )
    high, low = halves(table)
    both = jnp.concatenate([high, low], axis=1)
    last = got_ref[pl.ds(share * mine, groups, stride=chunk), :]
    for n in range(1, tiles // LANES):
        last = jnp.maximum(last, got_ref[pl.ds(share * mine + n, groups, stride=chunk), :])
    more_ref[0] = (jnp.max(last) >= usual).astype(jnp.int32)
    at = lax.broadcasted_iota(jnp.int32, (slots, tiles), 0).astype(jnp.float32)
    for g in range(groups):
        place = jnp.concatenate(
            [got_ref[pl.ds(g * chunk + share * mine + n, 1), :] for n in range(tiles // LANES)],
            axis=1,
        )
        hot_ref[pl.ds(g * slots, slots), :] = jnp.where(at == place, 1.0, 0.0).astype(jnp.bfloat16)
    width = share * LANES
    step = 512
    for b in range(groups * slots // step):
        sums = jnp.dot(
            hot_ref[pl.ds(b * step, step), :], both, preferred_element_type=jnp.float32
        )
        sums = sums[:, :width] + sums[:, width:]
        for g in range(step // slots):
            to = (b * step // slots + g) * share
            for r in range(share):
                mid = g * slots + usual
                lanes = slice(r * LANES, (r + 1) * LANES)
                out_ref[pl.ds((to + r) * usual, usual), :] = sums[g * slots : mid, lanes]
                rest_ref[pl.ds((to + r) * (slots - usual), slots - usual), :] = sums[
                    mid : (g + 1) * slots, lanes
                ]


def multiply(
    late, groups, half, mine, depth, rows, usual,
    par_hbm, src_hbm, cnt_hbm, irr_hbm, place_hbm, extra_ref, got_ref, int_ref, out_ref, turned_ref,
    par_ref, src_ref, cnt_ref, irr_ref, place_ref, term_ref, sems,
):
    pairs = [
        (src_hbm, src_ref), (cnt_hbm, cnt_ref), (irr_hbm, irr_ref), (place_hbm, place_ref),
        (par_hbm, par_ref),
    ]
    copies = [pltpu.make_async_copy(a, b, sems.at[n]) for n, (a, b) in enumerate(pairs)]
    for copy in copies:
        copy.start()
    share = rows // groups
    first = lax.axis_index("col") * mine
    other_first = lax.rem(lax.axis_index("col") + half, groups) * mine
    step = depth * LANES
    for m in range(mine):
        at = pl.ds(m * step, step)
        term_ref[at, :] = jnp.concatenate(halves(int_ref[at, :]), axis=1)
    for copy in copies:
        copy.wait()
    low, count = (usual, mine * depth - usual) if late else (0, usual)
    for m in range(mine):
        cols = []
        for k in range(depth):
            source = src_ref[m, k]
            place = place_ref[0, source]
            live = (k < cnt_ref[m]) & (irr_ref[source] == irr_ref[first + m])
            at = jnp.clip(place - low, 0, count - 1)
            block = jnp.concatenate(
                [
                    got_ref[pl.ds(r * count + at, groups, stride=share * count), :]
                    for r in range(share)
                ],
                axis=0,
            )
            if late:
                live = live & (place >= usual)
            else:
                live = live & (place < usual)
                owned = (source >= first) & (source < first + mine)
                own = jnp.where(owned, source - first, 0)
                own_block = extra_ref[:, pl.ds(pl.multiple_of(own * LANES, LANES), LANES)]
                block = jnp.where(owned, own_block, block)
            cols.append(jnp.where(live, block, 0.0))
        left_high, left_low = halves(jnp.concatenate(cols, axis=1))
        sums = jnp.dot(
            jnp.concatenate([left_high, left_low], axis=0),
            term_ref[pl.ds(m * step, step), :],
            preferred_element_type=jnp.float32,
        )
        sums = sums[:, :LANES] + sums[:, LANES:]
        sums = sums[:rows] + sums[rows:]
        if late:
            sums = sums + extra_ref[m]
        out_ref[m] = sums
        turned_ref[par_ref[first + m] - other_first] = sums


def finish(mine, rows, lad_ref, mir_ref, occ_ref, virt_ref, out_ref):
    row = lax.broadcasted_iota(jnp.int32, (rows, rows), 0)
    col = lax.broadcasted_iota(jnp.int32, (rows, rows), 1)
    occ = jnp.sum(jnp.where(row == col, occ_ref[...], 0.0), axis=1, keepdims=True)
    for m in range(mine):
        lanes = pl.ds(m * LANES, LANES)
        out_ref[:, lanes] = (lad_ref[m] + mir_ref[m]) / (occ - virt_ref[:, lanes])


def shards(amplitudes, integrals, sources, counts, tile_irrep, partner, occ_energy, virt_energy):
    rows = amplitudes.shape[0]
    mine, depth, width, _ = integrals.shape
    tiles = tile_irrep.shape[0]
    cols = lax.axis_size("col")
    heights = lax.axis_size("row")
    slots = mine * depth
    share = rows // cols
    chunk = share * mine + SUB
    f32 = jnp.float32

    i32 = jnp.int32
    usual = USUAL
    left = slots - usual

    def call(body, out, *args, specs, outs=None, scratch=(), flops=0, moved=0, room=16):
        return pl.pallas_call(
            body,
            out_shape=[jax.ShapeDtypeStruct(shape, dtype) for shape, dtype in out],
            in_specs=specs,
            out_specs=outs or [VMEM] * len(out),
            scratch_shapes=scratch,
            compiler_params=pltpu.CompilerParams(vmem_limit_bytes=room * 1024 * 1024),
            cost_estimate=pl.CostEstimate(flops=flops, bytes_accessed=moved, transcendentals=0),
        )(*args)

    sent, place = call(
        lambda *refs: spread(cols, mine, depth, rows, tiles, *refs),
        [((cols * chunk, LANES), f32), ((1, tiles), i32)],
        sources, counts, tile_irrep, tile_irrep.reshape(1, tiles), amplitudes,
        specs=[HBM] * 5,
        scratch=[
            pltpu.SMEM(sources.shape, i32),
            pltpu.SMEM(counts.shape, i32),
            pltpu.SMEM((tiles,), i32),
            pltpu.VMEM((1, tiles), i32),
            pltpu.VMEM(amplitudes.shape, f32),
            pltpu.SemaphoreType.DMA((5,)),
        ],
        moved=2 * amplitudes.size * 4,
        room=63,
    )
    got = lax.all_to_all(sent.reshape(cols, chunk, LANES), "col", 0, 0)
    sent, rest, more = call(
        lambda *refs: pick(cols, mine, slots, usual, share, tiles, *refs),
        [
            ((cols * share * usual, LANES), f32),
            ((cols * share * left, LANES), f32),
            ((1,), i32),
        ],
        got.reshape(cols * chunk, LANES),
        specs=[VMEM],
        outs=[VMEM, VMEM, SMEM],
        scratch=[pltpu.VMEM((cols * slots, tiles), jnp.bfloat16)],
        flops=4 * cols * slots * tiles * share * LANES,
        moved=cols * slots * share * LANES * 4,
    )
    got = lax.all_to_all(sent.reshape(cols, share * usual, LANES), "col", 0, 0)

    def products(late, extra, got):
        return call(
            lambda *refs: multiply(late, cols, cols // 2, mine, depth, rows, usual, *refs),
            [((mine, rows, width), f32)] * 2,
            partner, sources, counts, tile_irrep, place, extra, got.reshape(-1, LANES),
            integrals.reshape(mine * depth * width, width),
            specs=[HBM] * 5 + [VMEM] * 3,
            scratch=[
                pltpu.SMEM((tiles,), i32),
                pltpu.SMEM(sources.shape, i32),
                pltpu.SMEM(counts.shape, i32),
                pltpu.SMEM((tiles,), i32),
                pltpu.SMEM((1, tiles), i32),
                pltpu.VMEM((mine * depth * width, 2 * width), jnp.bfloat16),
                pltpu.SemaphoreType.DMA((5,)),
            ],
            flops=8 * rows * mine * depth * width * width,
            moved=integrals.size * 4 + got.size * 4,
        )

    pairs = [
        (r * cols + c, (r + heights // 2) % heights * cols + (c + cols // 2) % cols)
        for r in range(heights)
        for c in range(cols)
    ]

    def close(ladder, mirrored, rest):
        return call(
            lambda *refs: finish(mine, rows, *refs),
            [((rows, mine * width), f32)],
            ladder, mirrored, occ_energy.reshape(1, rows),
            virt_energy.reshape(1, mine * width),
            specs=[VMEM] * 4,
            moved=4 * rows * mine * width * 3,
        )[0]

    def amend(ladder, mirrored, rest):
        rest = lax.all_to_all(rest.reshape(cols, share * left, LANES), "col", 0, 0)
        ladder, turned = products(True, ladder, rest)
        return close(ladder, lax.ppermute(turned, ("row", "col"), pairs), rest)

    ladder, turned = products(False, amplitudes, got)
    more, turned = lax.optimization_barrier((more, turned))
    mirrored = lax.ppermute(turned, ("row", "col"), pairs)
    return lax.cond(more[0] > 0, amend, close, ladder, mirrored, rest)


def solution(mesh):
    placed = (
        P("row", "col"),
        P("col", None, None, None),
        P("col", None),
        P("col"),
        P(),
        P(),
        P("row"),
        P("col"),
    )
    return jax.shard_map(
        shards, mesh=mesh, in_specs=placed, out_specs=P("row", "col"), check_vma=False
    )
```

```python
import jax
import jax.numpy as jnp
from jax import lax
from jax.experimental import pallas as pl
from jax.experimental.pallas import tpu as pltpu
from jax.sharding import PartitionSpec as P

LANES = 128
SUB = 8
VMEM = pl.BlockSpec(memory_space=pltpu.VMEM)
HBM = pl.BlockSpec(memory_space=pltpu.HBM)
SMEM = pl.BlockSpec(memory_space=pltpu.SMEM)
USUAL = 55


def halves(x):
    high = x.astype(jnp.bfloat16)
    low = (x - high.astype(jnp.float32)).astype(jnp.bfloat16)
    return high, low


def spread(
    groups, mine, depth, rows, tiles,
    src_hbm, cnt_hbm, irr_hbm, row_hbm, amp_hbm, out_ref, place_ref,
    src_ref, cnt_ref, irr_ref, row_ref, amp_ref, sems,
):
    pairs = [
        (amp_hbm, amp_ref), (irr_hbm, irr_ref), (src_hbm, src_ref), (cnt_hbm, cnt_ref),
        (row_hbm, row_ref),
    ]
    copies = [pltpu.make_async_copy(a, b, sems.at[n]) for n, (a, b) in enumerate(pairs)]
    for copy in copies:
        copy.start()
    me = lax.axis_index("col")
    share = rows // groups
    chunk = share * mine + tiles // LANES
    before = lax.broadcasted_iota(jnp.int32, (tiles, tiles), 0)
    after = lax.broadcasted_iota(jnp.int32, (tiles, tiles), 1)
    earlier = jnp.where(before < after, 1.0, 0.0).astype(jnp.bfloat16)
    for copy in copies[1:]:
        copy.wait()
    tile = lax.broadcasted_iota(jnp.int32, (1, tiles), 1)
    label = row_ref[...] * tiles + tile
    listed = jnp.zeros((1, tiles), jnp.int32)
    for m in range(mine):
        base = irr_ref[me * mine + m] * tiles
        count = cnt_ref[m]
        for k in range(depth):
            key = jnp.where(k < count, src_ref[m, k] + base, -1)
            listed = jnp.where(label == key, 1, listed)
    owned = (tile >= me * mine) & (tile < me * mine + mine)
    listed = jnp.where(owned, 0, listed)
    rank = jnp.dot(
        jnp.broadcast_to(listed, (2 * SUB, tiles)).astype(jnp.float32).astype(jnp.bfloat16),
        earlier,
        preferred_element_type=jnp.float32,
    )[:1]
    place = jnp.where(listed > 0, rank, -1.0)
    place_ref[...] = place.astype(jnp.int32)
    line = lax.broadcasted_iota(jnp.int32, (SUB, LANES), 0)
    sheet = jnp.zeros((SUB, LANES), jnp.float32)
    for n in range(tiles // LANES):
        sheet = jnp.where(line == n, place[:, n * LANES : (n + 1) * LANES], sheet)
    for j in range(groups):
        out_ref[pl.ds(j * chunk + share * mine, tiles // LANES), :] = sheet[: tiles // LANES]
    copies[0].wait()
    for i in range(rows // SUB):
        r, j = divmod(i * SUB, groups)
        for m in range(mine):
            out_ref[pl.ds(j * chunk + r * mine + m, SUB, stride=chunk), :] = amp_ref[
                pl.ds(i * SUB, SUB), pl.ds(m * LANES, LANES)
            ]


def pick(groups, mine, slots, usual, share, tiles, got_ref, out_ref, rest_ref, more_ref, hot_ref):
    chunk = share * mine + tiles // LANES
    table = jnp.concatenate(
        [
            jnp.concatenate(
                [got_ref[pl.ds(g * chunk + r * mine, mine), :] for g in range(groups)], axis=0
            )
            for r in range(share)
        ],
        axis=1,
    )
    high, low = halves(table)
    both = jnp.concatenate([high, low], axis=1)
    last = got_ref[pl.ds(share * mine, groups, stride=chunk), :]
    for n in range(1, tiles // LANES):
        last = jnp.maximum(last, got_ref[pl.ds(share * mine + n, groups, stride=chunk), :])
    more_ref[0] = (jnp.max(last) >= usual).astype(jnp.int32)
    at = lax.broadcasted_iota(jnp.int32, (slots, tiles), 0).astype(jnp.float32)
    for g in range(groups):
        place = jnp.concatenate(
            [got_ref[pl.ds(g * chunk + share * mine + n, 1), :] for n in range(tiles // LANES)],
            axis=1,
        )
        hot_ref[pl.ds(g * slots, slots), :] = jnp.where(at == place, 1.0, 0.0).astype(jnp.bfloat16)
    width = share * LANES
    step = 512
    for b in range(groups * slots // step):
        sums = jnp.dot(
            hot_ref[pl.ds(b * step, step), :], both, preferred_element_type=jnp.float32
        )
        sums = sums[:, :width] + sums[:, width:]
        for g in range(step // slots):
            to = (b * step // slots + g) * share
            for r in range(share):
                mid = g * slots + usual
                lanes = slice(r * LANES, (r + 1) * LANES)
                out_ref[pl.ds((to + r) * usual, usual), :] = sums[g * slots : mid, lanes]
                rest_ref[pl.ds((to + r) * (slots - usual), slots - usual), :] = sums[
                    mid : (g + 1) * slots, lanes
                ]


def multiply(
    late, groups, half, mine, depth, rows, usual,
    par_hbm, src_hbm, cnt_hbm, irr_hbm, place_hbm, extra_ref, got_ref, int_ref, out_ref, turned_ref,
    par_ref, src_ref, cnt_ref, irr_ref, place_ref, term_ref, sems,
):
    pairs = [
        (src_hbm, src_ref), (cnt_hbm, cnt_ref), (irr_hbm, irr_ref), (place_hbm, place_ref),
        (par_hbm, par_ref),
    ]
    copies = [pltpu.make_async_copy(a, b, sems.at[n]) for n, (a, b) in enumerate(pairs)]
    for copy in copies:
        copy.start()
    share = rows // groups
    first = lax.axis_index("col") * mine
    other_first = lax.rem(lax.axis_index("col") + half, groups) * mine
    step = depth * LANES
    for m in range(mine):
        at = pl.ds(m * step, step)
        term_ref[at, :] = jnp.concatenate(halves(int_ref[at, :]), axis=1)
    for copy in copies:
        copy.wait()
    low, count = (usual, mine * depth - usual) if late else (0, usual)
    for m in range(mine):
        cols = []
        for k in range(depth):
            source = src_ref[m, k]
            place = place_ref[0, source]
            live = (k < cnt_ref[m]) & (irr_ref[source] == irr_ref[first + m])
            at = jnp.clip(place - low, 0, count - 1)
            block = jnp.concatenate(
                [
                    got_ref[pl.ds(r * count + at, groups, stride=share * count), :]
                    for r in range(share)
                ],
                axis=0,
            )
            if late:
                live = live & (place >= usual)
            else:
                live = live & (place < usual)
                owned = (source >= first) & (source < first + mine)
                own = jnp.where(owned, source - first, 0)
                own_block = extra_ref[:, pl.ds(pl.multiple_of(own * LANES, LANES), LANES)]
                block = jnp.where(owned, own_block, block)
            cols.append(jnp.where(live, block, 0.0))
        left_high, left_low = halves(jnp.concatenate(cols, axis=1))
        sums = jnp.dot(
            jnp.concatenate([left_high, left_low], axis=0),
            term_ref[pl.ds(m * step, step), :],
            preferred_element_type=jnp.float32,
        )
        sums = sums[:, :LANES] + sums[:, LANES:]
        sums = sums[:rows] + sums[rows:]
        if late:
            sums = sums + extra_ref[m]
        out_ref[m] = sums
        turned_ref[par_ref[first + m] - other_first] = sums


def finish(mine, rows, lad_ref, mir_ref, occ_ref, virt_ref, out_ref):
    row = lax.broadcasted_iota(jnp.int32, (rows, rows), 0)
    col = lax.broadcasted_iota(jnp.int32, (rows, rows), 1)
    occ = jnp.sum(jnp.where(row == col, occ_ref[...], 0.0), axis=1, keepdims=True)
    for m in range(mine):
        lanes = pl.ds(m * LANES, LANES)
        out_ref[:, lanes] = (lad_ref[m] + mir_ref[m]) / (occ - virt_ref[:, lanes])


def shards(amplitudes, integrals, sources, counts, tile_irrep, partner, occ_energy, virt_energy):
    rows = amplitudes.shape[0]
    mine, depth, width, _ = integrals.shape
    tiles = tile_irrep.shape[0]
    cols = lax.axis_size("col")
    heights = lax.axis_size("row")
    slots = mine * depth
    share = rows // cols
    chunk = share * mine + tiles // LANES
    f32 = jnp.float32

    i32 = jnp.int32
    usual = USUAL
    left = slots - usual

    def call(body, out, *args, specs, outs=None, scratch=(), flops=0, moved=0, room=16):
        return pl.pallas_call(
            body,
            out_shape=[jax.ShapeDtypeStruct(shape, dtype) for shape, dtype in out],
            in_specs=specs,
            out_specs=outs or [VMEM] * len(out),
            scratch_shapes=scratch,
            compiler_params=pltpu.CompilerParams(vmem_limit_bytes=room * 1024 * 1024),
            cost_estimate=pl.CostEstimate(flops=flops, bytes_accessed=moved, transcendentals=0),
        )(*args)

    sent, place = call(
        lambda *refs: spread(cols, mine, depth, rows, tiles, *refs),
        [((cols * chunk, LANES), f32), ((1, tiles), i32)],
        sources, counts, tile_irrep, tile_irrep.reshape(1, tiles), amplitudes,
        specs=[HBM] * 5,
        scratch=[
            pltpu.SMEM(sources.shape, i32),
            pltpu.SMEM(counts.shape, i32),
            pltpu.SMEM((tiles,), i32),
            pltpu.VMEM((1, tiles), i32),
            pltpu.VMEM(amplitudes.shape, f32),
            pltpu.SemaphoreType.DMA((5,)),
        ],
        moved=2 * amplitudes.size * 4,
        room=63,
    )
    got = lax.all_to_all(sent.reshape(cols, chunk, 1, LANES), "col", 0, 0)
    sent, rest, more = call(
        lambda *refs: pick(cols, mine, slots, usual, share, tiles, *refs),
        [
            ((cols * share * usual, LANES), f32),
            ((cols * share * left, LANES), f32),
            ((1,), i32),
        ],
        got.reshape(cols * chunk, LANES),
        specs=[VMEM],
        outs=[VMEM, VMEM, SMEM],
        scratch=[pltpu.VMEM((cols * slots, tiles), jnp.bfloat16)],
        flops=4 * cols * slots * tiles * share * LANES,
        moved=cols * slots * share * LANES * 4,
    )
    got = lax.all_to_all(sent.reshape(cols, share * usual, 1, LANES), "col", 0, 0)

    def products(late, extra, got):
        return call(
            lambda *refs: multiply(late, cols, cols // 2, mine, depth, rows, usual, *refs),
            [((mine, rows, width), f32)] * 2,
            partner, sources, counts, tile_irrep, place, extra, got.reshape(-1, LANES),
            integrals.reshape(mine * depth * width, width),
            specs=[HBM] * 5 + [VMEM] * 3,
            scratch=[
                pltpu.SMEM((tiles,), i32),
                pltpu.SMEM(sources.shape, i32),
                pltpu.SMEM(counts.shape, i32),
                pltpu.SMEM((tiles,), i32),
                pltpu.SMEM((1, tiles), i32),
                pltpu.VMEM((mine * depth * width, 2 * width), jnp.bfloat16),
                pltpu.SemaphoreType.DMA((5,)),
            ],
            flops=8 * rows * mine * depth * width * width,
            moved=integrals.size * 4 + got.size * 4,
        )

    pairs = [
        (r * cols + c, (r + heights // 2) % heights * cols + (c + cols // 2) % cols)
        for r in range(heights)
        for c in range(cols)
    ]

    def close(ladder, mirrored, rest):
        return call(
            lambda *refs: finish(mine, rows, *refs),
            [((rows, mine * width), f32)],
            ladder, mirrored, occ_energy.reshape(1, rows),
            virt_energy.reshape(1, mine * width),
            specs=[VMEM] * 4,
            moved=4 * rows * mine * width * 3,
        )[0]

    def amend(ladder, mirrored, rest):
        rest = lax.all_to_all(rest.reshape(cols, share * left, 1, LANES), "col", 0, 0)
        ladder, turned = products(True, ladder, rest)
        return close(ladder, lax.ppermute(turned, ("row", "col"), pairs), rest)

    ladder, turned = products(False, amplitudes, got)
    more, turned = lax.optimization_barrier((more, turned))
    mirrored = lax.ppermute(turned, ("row", "col"), pairs)
    return lax.cond(more[0] > 0, amend, close, ladder, mirrored, rest)


def solution(mesh):
    placed = (
        P("row", "col"),
        P("col", None, None, None),
        P("col", None),
        P("col"),
        P(),
        P(),
        P("row"),
        P("col"),
    )
    return jax.shard_map(
        shards, mesh=mesh, in_specs=placed, out_specs=P("row", "col"), check_vma=False
    )
```

```python
import jax
import jax.numpy as jnp
from jax import lax
from jax.experimental import pallas as pl
from jax.experimental.pallas import tpu as pltpu
from jax.sharding import PartitionSpec as P

LANES = 128
SUB = 8
VMEM = pl.BlockSpec(memory_space=pltpu.VMEM)
HBM = pl.BlockSpec(memory_space=pltpu.HBM)
SMEM = pl.BlockSpec(memory_space=pltpu.SMEM)
USUAL = 55


def halves(x):
    high = x.astype(jnp.bfloat16)
    low = (x - high.astype(jnp.float32)).astype(jnp.bfloat16)
    return high, low


def spread(
    groups, mine, depth, rows, tiles,
    src_hbm, cnt_hbm, irr_hbm, row_hbm, amp_hbm, out_ref, place_ref,
    src_ref, cnt_ref, irr_ref, row_ref, amp_ref, sems,
):
    pairs = [
        (irr_hbm, irr_ref), (src_hbm, src_ref), (cnt_hbm, cnt_ref), (row_hbm, row_ref),
        (amp_hbm, amp_ref),
    ]
    copies = [pltpu.make_async_copy(a, b, sems.at[n]) for n, (a, b) in enumerate(pairs)]
    for copy in copies:
        copy.start()
    me = lax.axis_index("col")
    share = rows // groups
    chunk = share * mine + tiles // LANES
    before = lax.broadcasted_iota(jnp.int32, (tiles, tiles), 0)
    after = lax.broadcasted_iota(jnp.int32, (tiles, tiles), 1)
    earlier = jnp.where(before < after, 1.0, 0.0).astype(jnp.bfloat16)
    for copy in copies[:4]:
        copy.wait()
    tile = lax.broadcasted_iota(jnp.int32, (1, tiles), 1)
    label = row_ref[...] * tiles + tile
    listed = jnp.zeros((1, tiles), jnp.int32)
    for m in range(mine):
        base = irr_ref[me * mine + m] * tiles
        count = cnt_ref[m]
        for k in range(depth):
            key = jnp.where(k < count, src_ref[m, k] + base, -1)
            listed = jnp.where(label == key, 1, listed)
    owned = (tile >= me * mine) & (tile < me * mine + mine)
    listed = jnp.where(owned, 0, listed)
    rank = jnp.dot(
        jnp.broadcast_to(listed, (2 * SUB, tiles)).astype(jnp.float32).astype(jnp.bfloat16),
        earlier,
        preferred_element_type=jnp.float32,
    )[:1]
    place = jnp.where(listed > 0, rank, -1.0)
    place_ref[...] = place.astype(jnp.int32)
    line = lax.broadcasted_iota(jnp.int32, (SUB, LANES), 0)
    sheet = jnp.zeros((SUB, LANES), jnp.float32)
    for n in range(tiles // LANES):
        sheet = jnp.where(line == n, place[:, n * LANES : (n + 1) * LANES], sheet)
    for j in range(groups):
        out_ref[pl.ds(j * chunk + share * mine, tiles // LANES), :] = sheet[: tiles // LANES]
    copies[4].wait()
    for i in range(rows // SUB):
        r, j = divmod(i * SUB, groups)
        for m in range(mine):
            out_ref[pl.ds(j * chunk + r * mine + m, SUB, stride=chunk), :] = amp_ref[
                pl.ds(i * SUB, SUB), pl.ds(m * LANES, LANES)
            ]


def pick(groups, mine, slots, usual, share, tiles, got_ref, out_ref, rest_ref, more_ref, hot_ref):
    chunk = share * mine + tiles // LANES
    table = jnp.concatenate(
        [
            jnp.concatenate(
                [got_ref[pl.ds(g * chunk + r * mine, mine), :] for g in range(groups)], axis=0
            )
            for r in range(share)
        ],
        axis=1,
    )
    high, low = halves(table)
    both = jnp.concatenate([high, low], axis=1)
    last = got_ref[pl.ds(share * mine, groups, stride=chunk), :]
    for n in range(1, tiles // LANES):
        last = jnp.maximum(last, got_ref[pl.ds(share * mine + n, groups, stride=chunk), :])
    more_ref[0] = (jnp.max(last) >= usual).astype(jnp.int32)
    at = lax.broadcasted_iota(jnp.int32, (slots, tiles), 0).astype(jnp.float32)
    for g in range(groups):
        place = jnp.concatenate(
            [got_ref[pl.ds(g * chunk + share * mine + n, 1), :] for n in range(tiles // LANES)],
            axis=1,
        )
        hot_ref[pl.ds(g * slots, slots), :] = jnp.where(at == place, 1.0, 0.0).astype(jnp.bfloat16)
    width = share * LANES
    step = 512
    for b in range(groups * slots // step):
        sums = jnp.dot(
            hot_ref[pl.ds(b * step, step), :], both, preferred_element_type=jnp.float32
        )
        sums = sums[:, :width] + sums[:, width:]
        for g in range(step // slots):
            to = (b * step // slots + g) * share
            for r in range(share):
                mid = g * slots + usual
                lanes = slice(r * LANES, (r + 1) * LANES)
                out_ref[pl.ds((to + r) * usual, usual), :] = sums[g * slots : mid, lanes]
                rest_ref[pl.ds((to + r) * (slots - usual), slots - usual), :] = sums[
                    mid : (g + 1) * slots, lanes
                ]


def multiply(
    late, groups, half, mine, depth, rows, usual,
    par_hbm, src_hbm, cnt_hbm, irr_hbm, place_hbm, extra_ref, got_ref, int_ref, out_ref, turned_ref,
    par_ref, src_ref, cnt_ref, irr_ref, place_ref, term_ref, sems,
):
    pairs = [
        (src_hbm, src_ref), (cnt_hbm, cnt_ref), (irr_hbm, irr_ref), (place_hbm, place_ref),
        (par_hbm, par_ref),
    ]
    copies = [pltpu.make_async_copy(a, b, sems.at[n]) for n, (a, b) in enumerate(pairs)]
    for copy in copies:
        copy.start()
    share = rows // groups
    first = lax.axis_index("col") * mine
    other_first = lax.rem(lax.axis_index("col") + half, groups) * mine
    step = depth * LANES
    for m in range(mine):
        at = pl.ds(m * step, step)
        term_ref[at, :] = jnp.concatenate(halves(int_ref[at, :]), axis=1)
    for copy in copies:
        copy.wait()
    low, count = (usual, mine * depth - usual) if late else (0, usual)
    for m in range(mine):
        cols = []
        for k in range(depth):
            source = src_ref[m, k]
            place = place_ref[0, source]
            live = (k < cnt_ref[m]) & (irr_ref[source] == irr_ref[first + m])
            at = jnp.clip(place - low, 0, count - 1)
            block = jnp.concatenate(
                [
                    got_ref[pl.ds(r * count + at, groups, stride=share * count), :]
                    for r in range(share)
                ],
                axis=0,
            )
            if late:
                live = live & (place >= usual)
            else:
                live = live & (place < usual)
                owned = (source >= first) & (source < first + mine)
                own = jnp.where(owned, source - first, 0)
                own_block = extra_ref[:, pl.ds(pl.multiple_of(own * LANES, LANES), LANES)]
                block = jnp.where(owned, own_block, block)
            cols.append(jnp.where(live, block, 0.0))
        left_high, left_low = halves(jnp.concatenate(cols, axis=1))
        sums = jnp.dot(
            jnp.concatenate([left_high, left_low], axis=0),
            term_ref[pl.ds(m * step, step), :],
            preferred_element_type=jnp.float32,
        )
        sums = sums[:, :LANES] + sums[:, LANES:]
        sums = sums[:rows] + sums[rows:]
        if late:
            sums = sums + extra_ref[m]
        out_ref[m] = sums
        turned_ref[par_ref[first + m] - other_first] = sums


def finish(mine, rows, lad_ref, mir_ref, occ_ref, virt_ref, out_ref):
    row = lax.broadcasted_iota(jnp.int32, (rows, rows), 0)
    col = lax.broadcasted_iota(jnp.int32, (rows, rows), 1)
    occ = jnp.sum(jnp.where(row == col, occ_ref[...], 0.0), axis=1, keepdims=True)
    for m in range(mine):
        lanes = pl.ds(m * LANES, LANES)
        out_ref[:, lanes] = (lad_ref[m] + mir_ref[m]) / (occ - virt_ref[:, lanes])


def shards(amplitudes, integrals, sources, counts, tile_irrep, partner, occ_energy, virt_energy):
    rows = amplitudes.shape[0]
    mine, depth, width, _ = integrals.shape
    tiles = tile_irrep.shape[0]
    cols = lax.axis_size("col")
    heights = lax.axis_size("row")
    slots = mine * depth
    share = rows // cols
    chunk = share * mine + tiles // LANES
    f32 = jnp.float32

    i32 = jnp.int32
    usual = USUAL
    left = slots - usual

    def call(body, out, *args, specs, outs=None, scratch=(), flops=0, moved=0, room=16):
        return pl.pallas_call(
            body,
            out_shape=[jax.ShapeDtypeStruct(shape, dtype) for shape, dtype in out],
            in_specs=specs,
            out_specs=outs or [VMEM] * len(out),
            scratch_shapes=scratch,
            compiler_params=pltpu.CompilerParams(vmem_limit_bytes=room * 1024 * 1024),
            cost_estimate=pl.CostEstimate(flops=flops, bytes_accessed=moved, transcendentals=0),
        )(*args)

    sent, place = call(
        lambda *refs: spread(cols, mine, depth, rows, tiles, *refs),
        [((cols * chunk, LANES), f32), ((1, tiles), i32)],
        sources, counts, tile_irrep, tile_irrep.reshape(1, tiles), amplitudes,
        specs=[HBM] * 5,
        scratch=[
            pltpu.SMEM(sources.shape, i32),
            pltpu.SMEM(counts.shape, i32),
            pltpu.SMEM((tiles,), i32),
            pltpu.VMEM((1, tiles), i32),
            pltpu.VMEM(amplitudes.shape, f32),
            pltpu.SemaphoreType.DMA((5,)),
        ],
        moved=2 * amplitudes.size * 4,
        room=63,
    )
    got = lax.all_to_all(sent.reshape(cols, chunk, 1, LANES), "col", 0, 0)
    sent, rest, more = call(
        lambda *refs: pick(cols, mine, slots, usual, share, tiles, *refs),
        [
            ((cols * share * usual, LANES), f32),
            ((cols * share * left, LANES), f32),
            ((1,), i32),
        ],
        got.reshape(cols * chunk, LANES),
        specs=[VMEM],
        outs=[VMEM, VMEM, SMEM],
        scratch=[pltpu.VMEM((cols * slots, tiles), jnp.bfloat16)],
        flops=4 * cols * slots * tiles * share * LANES,
        moved=cols * slots * share * LANES * 4,
    )
    got = lax.all_to_all(sent.reshape(cols, share * usual, 1, LANES), "col", 0, 0)

    def products(late, extra, got):
        return call(
            lambda *refs: multiply(late, cols, cols // 2, mine, depth, rows, usual, *refs),
            [((mine, rows, width), f32)] * 2,
            partner, sources, counts, tile_irrep, place, extra, got.reshape(-1, LANES),
            integrals.reshape(mine * depth * width, width),
            specs=[HBM] * 5 + [VMEM] * 3,
            scratch=[
                pltpu.SMEM((tiles,), i32),
                pltpu.SMEM(sources.shape, i32),
                pltpu.SMEM(counts.shape, i32),
                pltpu.SMEM((tiles,), i32),
                pltpu.SMEM((1, tiles), i32),
                pltpu.VMEM((mine * depth * width, 2 * width), jnp.bfloat16),
                pltpu.SemaphoreType.DMA((5,)),
            ],
            flops=8 * rows * mine * depth * width * width,
            moved=integrals.size * 4 + got.size * 4,
        )

    pairs = [
        (r * cols + c, (r + heights // 2) % heights * cols + (c + cols // 2) % cols)
        for r in range(heights)
        for c in range(cols)
    ]

    def close(ladder, mirrored, rest):
        return call(
            lambda *refs: finish(mine, rows, *refs),
            [((rows, mine * width), f32)],
            ladder, mirrored, occ_energy.reshape(1, rows),
            virt_energy.reshape(1, mine * width),
            specs=[VMEM] * 4,
            moved=4 * rows * mine * width * 3,
        )[0]

    def amend(ladder, mirrored, rest):
        rest = lax.all_to_all(rest.reshape(cols, share * left, 1, LANES), "col", 0, 0)
        ladder, turned = products(True, ladder, rest)
        return close(ladder, lax.ppermute(turned, ("row", "col"), pairs), rest)

    ladder, turned = products(False, amplitudes, got)
    more, turned = lax.optimization_barrier((more, turned))
    mirrored = lax.ppermute(turned, ("row", "col"), pairs)
    return lax.cond(more[0] > 0, amend, close, ladder, mirrored, rest)


def solution(mesh):
    placed = (
        P("row", "col"),
        P("col", None, None, None),
        P("col", None),
        P("col"),
        P(),
        P(),
        P("row"),
        P("col"),
    )
    return jax.shard_map(
        shards, mesh=mesh, in_specs=placed, out_specs=P("row", "col"), check_vma=False
    )
```

```python
import jax
import jax.numpy as jnp
from jax import lax
from jax.experimental import pallas as pl
from jax.experimental.pallas import tpu as pltpu
from jax.sharding import PartitionSpec as P

LANES = 128
SUB = 8
VMEM = pl.BlockSpec(memory_space=pltpu.VMEM)
HBM = pl.BlockSpec(memory_space=pltpu.HBM)
SMEM = pl.BlockSpec(memory_space=pltpu.SMEM)
USUAL = 53


def halves(x):
    high = x.astype(jnp.bfloat16)
    low = (x - high.astype(jnp.float32)).astype(jnp.bfloat16)
    return high, low


def spread(
    groups, mine, depth, rows, tiles,
    src_hbm, cnt_hbm, irr_hbm, row_hbm, amp_hbm, out_ref, place_ref,
    src_ref, cnt_ref, irr_ref, row_ref, amp_ref, sems,
):
    pairs = [
        (irr_hbm, irr_ref), (src_hbm, src_ref), (cnt_hbm, cnt_ref), (row_hbm, row_ref),
        (amp_hbm, amp_ref),
    ]
    copies = [pltpu.make_async_copy(a, b, sems.at[n]) for n, (a, b) in enumerate(pairs)]
    for copy in copies:
        copy.start()
    me = lax.axis_index("col")
    share = rows // groups
    chunk = share * mine + tiles // LANES
    before = lax.broadcasted_iota(jnp.int32, (tiles, tiles), 0)
    after = lax.broadcasted_iota(jnp.int32, (tiles, tiles), 1)
    earlier = jnp.where(before < after, 1.0, 0.0).astype(jnp.bfloat16)
    for copy in copies[:4]:
        copy.wait()
    tile = lax.broadcasted_iota(jnp.int32, (1, tiles), 1)
    label = row_ref[...] * tiles + tile
    listed = jnp.zeros((1, tiles), jnp.int32)
    for m in range(mine):
        base = irr_ref[me * mine + m] * tiles
        count = cnt_ref[m]
        for k in range(depth):
            key = jnp.where(k < count, src_ref[m, k] + base, -1)
            listed = jnp.where(label == key, 1, listed)
    owned = (tile >= me * mine) & (tile < me * mine + mine)
    listed = jnp.where(owned, 0, listed)
    rank = jnp.dot(
        jnp.broadcast_to(listed, (2 * SUB, tiles)).astype(jnp.float32).astype(jnp.bfloat16),
        earlier,
        preferred_element_type=jnp.float32,
    )[:1]
    place = jnp.where(listed > 0, rank, -1.0)
    place_ref[...] = place.astype(jnp.int32)
    line = lax.broadcasted_iota(jnp.int32, (SUB, LANES), 0)
    sheet = jnp.zeros((SUB, LANES), jnp.float32)
    for n in range(tiles // LANES):
        sheet = jnp.where(line == n, place[:, n * LANES : (n + 1) * LANES], sheet)
    for j in range(groups):
        out_ref[pl.ds(j * chunk + share * mine, tiles // LANES), :] = sheet[: tiles // LANES]
    copies[4].wait()
    for i in range(rows // SUB):
        r, j = divmod(i * SUB, groups)
        for m in range(mine):
            out_ref[pl.ds(j * chunk + r * mine + m, SUB, stride=chunk), :] = amp_ref[
                pl.ds(i * SUB, SUB), pl.ds(m * LANES, LANES)
            ]


def pick(groups, mine, slots, usual, share, tiles, got_ref, out_ref, rest_ref, more_ref, hot_ref):
    chunk = share * mine + tiles // LANES
    table = jnp.concatenate(
        [
            jnp.concatenate(
                [got_ref[pl.ds(g * chunk + r * mine, mine), :] for g in range(groups)], axis=0
            )
            for r in range(share)
        ],
        axis=1,
    )
    high, low = halves(table)
    both = jnp.concatenate([high, low], axis=1)
    last = got_ref[pl.ds(share * mine, groups, stride=chunk), :]
    for n in range(1, tiles // LANES):
        last = jnp.maximum(last, got_ref[pl.ds(share * mine + n, groups, stride=chunk), :])
    more_ref[0] = (jnp.max(last) >= usual).astype(jnp.int32)
    at = lax.broadcasted_iota(jnp.int32, (slots, tiles), 0).astype(jnp.float32)
    for g in range(groups):
        place = jnp.concatenate(
            [got_ref[pl.ds(g * chunk + share * mine + n, 1), :] for n in range(tiles // LANES)],
            axis=1,
        )
        hot_ref[pl.ds(g * slots, slots), :] = jnp.where(at == place, 1.0, 0.0).astype(jnp.bfloat16)
    width = share * LANES
    step = 512
    for b in range(groups * slots // step):
        sums = jnp.dot(
            hot_ref[pl.ds(b * step, step), :], both, preferred_element_type=jnp.float32
        )
        sums = sums[:, :width] + sums[:, width:]
        for g in range(step // slots):
            to = (b * step // slots + g) * share
            for r in range(share):
                mid = g * slots + usual
                lanes = slice(r * LANES, (r + 1) * LANES)
                out_ref[pl.ds((to + r) * usual, usual), :] = sums[g * slots : mid, lanes]
                rest_ref[pl.ds((to + r) * (slots - usual), slots - usual), :] = sums[
                    mid : (g + 1) * slots, lanes
                ]


def multiply(
    late, groups, half, mine, depth, rows, usual,
    par_hbm, src_hbm, cnt_hbm, irr_hbm, place_hbm, extra_ref, got_ref, int_ref, out_ref, turned_ref,
    par_ref, src_ref, cnt_ref, irr_ref, place_ref, term_ref, sems,
):
    pairs = [
        (src_hbm, src_ref), (cnt_hbm, cnt_ref), (irr_hbm, irr_ref), (place_hbm, place_ref),
        (par_hbm, par_ref),
    ]
    copies = [pltpu.make_async_copy(a, b, sems.at[n]) for n, (a, b) in enumerate(pairs)]
    for copy in copies:
        copy.start()
    share = rows // groups
    first = lax.axis_index("col") * mine
    other_first = lax.rem(lax.axis_index("col") + half, groups) * mine
    step = depth * LANES
    for m in range(mine):
        at = pl.ds(m * step, step)
        term_ref[at, :] = jnp.concatenate(halves(int_ref[at, :]), axis=1)
    for copy in copies:
        copy.wait()
    low, count = (usual, mine * depth - usual) if late else (0, usual)
    for m in range(mine):
        cols = []
        for k in range(depth):
            source = src_ref[m, k]
            place = place_ref[0, source]
            live = (k < cnt_ref[m]) & (irr_ref[source] == irr_ref[first + m])
            at = jnp.clip(place - low, 0, count - 1)
            block = jnp.concatenate(
                [
                    got_ref[pl.ds(r * count + at, groups, stride=share * count), :]
                    for r in range(share)
                ],
                axis=0,
            )
            if late:
                live = live & (place >= usual)
            else:
                live = live & (place < usual)
                owned = (source >= first) & (source < first + mine)
                own = jnp.where(owned, source - first, 0)
                own_block = extra_ref[:, pl.ds(pl.multiple_of(own * LANES, LANES), LANES)]
                block = jnp.where(owned, own_block, block)
            cols.append(jnp.where(live, block, 0.0))
        left_high, left_low = halves(jnp.concatenate(cols, axis=1))
        sums = jnp.dot(
            jnp.concatenate([left_high, left_low], axis=0),
            term_ref[pl.ds(m * step, step), :],
            preferred_element_type=jnp.float32,
        )
        sums = sums[:, :LANES] + sums[:, LANES:]
        sums = sums[:rows] + sums[rows:]
        if late:
            sums = sums + extra_ref[m]
        out_ref[m] = sums
        turned_ref[par_ref[first + m] - other_first] = sums


def finish(mine, rows, lad_ref, mir_ref, occ_ref, virt_ref, out_ref):
    row = lax.broadcasted_iota(jnp.int32, (rows, rows), 0)
    col = lax.broadcasted_iota(jnp.int32, (rows, rows), 1)
    occ = jnp.sum(jnp.where(row == col, occ_ref[...], 0.0), axis=1, keepdims=True)
    for m in range(mine):
        lanes = pl.ds(m * LANES, LANES)
        out_ref[:, lanes] = (lad_ref[m] + mir_ref[m]) / (occ - virt_ref[:, lanes])


def shards(amplitudes, integrals, sources, counts, tile_irrep, partner, occ_energy, virt_energy):
    rows = amplitudes.shape[0]
    mine, depth, width, _ = integrals.shape
    tiles = tile_irrep.shape[0]
    cols = lax.axis_size("col")
    heights = lax.axis_size("row")
    slots = mine * depth
    share = rows // cols
    chunk = share * mine + tiles // LANES
    f32 = jnp.float32

    i32 = jnp.int32
    usual = USUAL
    left = slots - usual

    def call(body, out, *args, specs, outs=None, scratch=(), flops=0, moved=0, room=16):
        return pl.pallas_call(
            body,
            out_shape=[jax.ShapeDtypeStruct(shape, dtype) for shape, dtype in out],
            in_specs=specs,
            out_specs=outs or [VMEM] * len(out),
            scratch_shapes=scratch,
            compiler_params=pltpu.CompilerParams(vmem_limit_bytes=room * 1024 * 1024),
            cost_estimate=pl.CostEstimate(flops=flops, bytes_accessed=moved, transcendentals=0),
        )(*args)

    sent, place = call(
        lambda *refs: spread(cols, mine, depth, rows, tiles, *refs),
        [((cols * chunk, LANES), f32), ((1, tiles), i32)],
        sources, counts, tile_irrep, tile_irrep.reshape(1, tiles), amplitudes,
        specs=[HBM] * 5,
        scratch=[
            pltpu.SMEM(sources.shape, i32),
            pltpu.SMEM(counts.shape, i32),
            pltpu.SMEM((tiles,), i32),
            pltpu.VMEM((1, tiles), i32),
            pltpu.VMEM(amplitudes.shape, f32),
            pltpu.SemaphoreType.DMA((5,)),
        ],
        moved=2 * amplitudes.size * 4,
        room=63,
    )
    got = lax.all_to_all(sent.reshape(cols, chunk, 1, LANES), "col", 0, 0)
    sent, rest, more = call(
        lambda *refs: pick(cols, mine, slots, usual, share, tiles, *refs),
        [
            ((cols * share * usual, LANES), f32),
            ((cols * share * left, LANES), f32),
            ((1,), i32),
        ],
        got.reshape(cols * chunk, LANES),
        specs=[VMEM],
        outs=[VMEM, VMEM, SMEM],
        scratch=[pltpu.VMEM((cols * slots, tiles), jnp.bfloat16)],
        flops=4 * cols * slots * tiles * share * LANES,
        moved=cols * slots * share * LANES * 4,
    )
    got = lax.all_to_all(sent.reshape(cols, share * usual, 1, LANES), "col", 0, 0)

    def products(late, extra, got):
        return call(
            lambda *refs: multiply(late, cols, cols // 2, mine, depth, rows, usual, *refs),
            [((mine, rows, width), f32)] * 2,
            partner, sources, counts, tile_irrep, place, extra, got.reshape(-1, LANES),
            integrals.reshape(mine * depth * width, width),
            specs=[HBM] * 5 + [VMEM] * 3,
            scratch=[
                pltpu.SMEM((tiles,), i32),
                pltpu.SMEM(sources.shape, i32),
                pltpu.SMEM(counts.shape, i32),
                pltpu.SMEM((tiles,), i32),
                pltpu.SMEM((1, tiles), i32),
                pltpu.VMEM((mine * depth * width, 2 * width), jnp.bfloat16),
                pltpu.SemaphoreType.DMA((5,)),
            ],
            flops=8 * rows * mine * depth * width * width,
            moved=integrals.size * 4 + got.size * 4,
        )

    pairs = [
        (r * cols + c, (r + heights // 2) % heights * cols + (c + cols // 2) % cols)
        for r in range(heights)
        for c in range(cols)
    ]

    def close(ladder, mirrored, rest):
        return call(
            lambda *refs: finish(mine, rows, *refs),
            [((rows, mine * width), f32)],
            ladder, mirrored, occ_energy.reshape(1, rows),
            virt_energy.reshape(1, mine * width),
            specs=[VMEM] * 4,
            moved=4 * rows * mine * width * 3,
        )[0]

    def amend(ladder, mirrored, rest):
        rest = lax.all_to_all(rest.reshape(cols, share * left, 1, LANES), "col", 0, 0)
        ladder, turned = products(True, ladder, rest)
        return close(ladder, lax.ppermute(turned, ("row", "col"), pairs), rest)

    ladder, turned = products(False, amplitudes, got)
    more, turned = lax.optimization_barrier((more, turned))
    mirrored = lax.ppermute(turned, ("row", "col"), pairs)
    return lax.cond(more[0] > 0, amend, close, ladder, mirrored, rest)


def solution(mesh):
    placed = (
        P("row", "col"),
        P("col", None, None, None),
        P("col", None),
        P("col"),
        P(),
        P(),
        P("row"),
        P("col"),
    )
    return jax.shard_map(
        shards, mesh=mesh, in_specs=placed, out_specs=P("row", "col"), check_vma=False
    )
```

```python
import functools

import jax
import jax.numpy as jnp
from jax import lax
from jax.experimental import pallas as pl
from jax.experimental.pallas import tpu as pltpu
from jax.sharding import PartitionSpec as P

LANES = 128
SUB = 8
VMEM = pl.BlockSpec(memory_space=pltpu.VMEM)
HBM = pl.BlockSpec(memory_space=pltpu.HBM)
SMEM = pl.BlockSpec(memory_space=pltpu.SMEM)
USUAL = 55


def halves(x):
    high = x.astype(jnp.bfloat16)
    low = (x - high.astype(jnp.float32)).astype(jnp.bfloat16)
    return high, low


def spread(
    groups, mine, depth, rows, tiles,
    src_hbm, cnt_hbm, irr_hbm, row_hbm, amp_hbm, out_ref, place_ref,
    src_ref, cnt_ref, irr_ref, row_ref, amp_ref, sems,
):
    pairs = [
        (irr_hbm, irr_ref), (src_hbm, src_ref), (cnt_hbm, cnt_ref), (row_hbm, row_ref),
        (amp_hbm, amp_ref),
    ]
    copies = [pltpu.make_async_copy(a, b, sems.at[n]) for n, (a, b) in enumerate(pairs)]
    for copy in copies:
        copy.start()
    me = lax.axis_index("col")
    share = rows // groups
    chunk = share * mine + tiles // LANES
    before = lax.broadcasted_iota(jnp.int32, (tiles, tiles), 0)
    after = lax.broadcasted_iota(jnp.int32, (tiles, tiles), 1)
    earlier = jnp.where(before < after, 1.0, 0.0).astype(jnp.bfloat16)
    for copy in copies[:4]:
        copy.wait()
    tile = lax.broadcasted_iota(jnp.int32, (1, tiles), 1)
    label = row_ref[...] * tiles + tile
    listed = jnp.zeros((1, tiles), jnp.int32)
    for m in range(mine):
        base = irr_ref[me * mine + m] * tiles
        count = cnt_ref[m]
        for k in range(depth):
            key = jnp.where(k < count, src_ref[m, k] + base, -1)
            listed = jnp.where(label == key, 1, listed)
    owned = (tile >= me * mine) & (tile < me * mine + mine)
    listed = jnp.where(owned, 0, listed)
    rank = jnp.dot(
        jnp.broadcast_to(listed, (2 * SUB, tiles)).astype(jnp.float32).astype(jnp.bfloat16),
        earlier,
        preferred_element_type=jnp.float32,
    )[:1]
    place = jnp.where(listed > 0, rank, -1.0)
    place_ref[...] = place.astype(jnp.int32)
    line = lax.broadcasted_iota(jnp.int32, (SUB, LANES), 0)
    sheet = jnp.zeros((SUB, LANES), jnp.float32)
    for n in range(tiles // LANES):
        sheet = jnp.where(line == n, place[:, n * LANES : (n + 1) * LANES], sheet)
    for j in range(groups):
        out_ref[pl.ds(j * chunk + share * mine, tiles // LANES), :] = sheet[: tiles // LANES]
    copies[4].wait()
    for i in range(rows // SUB):
        r, j = divmod(i * SUB, groups)
        for m in range(mine):
            out_ref[pl.ds(j * chunk + r * mine + m, SUB, stride=chunk), :] = amp_ref[
                pl.ds(i * SUB, SUB), pl.ds(m * LANES, LANES)
            ]


def pick(groups, mine, slots, usual, share, tiles, got_ref, out_ref, rest_ref, more_ref, hot_ref):
    chunk = share * mine + tiles // LANES
    table = jnp.concatenate(
        [
            jnp.concatenate(
                [got_ref[pl.ds(g * chunk + r * mine, mine), :] for g in range(groups)], axis=0
            )
            for r in range(share)
        ],
        axis=1,
    )
    high, low = halves(table)
    both = jnp.concatenate([high, low], axis=1)
    last = got_ref[pl.ds(share * mine, groups, stride=chunk), :]
    for n in range(1, tiles // LANES):
        last = jnp.maximum(last, got_ref[pl.ds(share * mine + n, groups, stride=chunk), :])
    more = jnp.max(last) >= usual
    more_ref[0] = more.astype(jnp.int32)
    at = lax.broadcasted_iota(jnp.int32, (slots, tiles), 0).astype(jnp.float32)
    for g in range(groups):
        place = jnp.concatenate(
            [got_ref[pl.ds(g * chunk + share * mine + n, 1), :] for n in range(tiles // LANES)],
            axis=1,
        )
        hot_ref[pl.ds(g * slots, slots), :] = jnp.where(at == place, 1.0, 0.0).astype(jnp.bfloat16)
    width = share * LANES
    step = 512
    for b in range(groups * slots // step):
        sums = jnp.dot(
            hot_ref[pl.ds(b * step, step), :], both, preferred_element_type=jnp.float32
        )
        sums = sums[:, :width] + sums[:, width:]
        def keep(ref, low, high):
            for g in range(step // slots):
                to = (b * step // slots + g) * share
                for r in range(share):
                    ref[pl.ds((to + r) * (high - low), high - low), :] = sums[
                        g * slots + low : g * slots + high, r * LANES : (r + 1) * LANES
                    ]

        keep(out_ref, 0, usual)
        pl.when(more)(functools.partial(keep, rest_ref, usual, slots))


def multiply(
    late, groups, half, mine, depth, rows, usual,
    par_hbm, src_hbm, cnt_hbm, irr_hbm, place_hbm, extra_ref, got_ref, int_ref, out_ref, turned_ref,
    par_ref, src_ref, cnt_ref, irr_ref, place_ref, term_ref, sems,
):
    pairs = [
        (src_hbm, src_ref), (cnt_hbm, cnt_ref), (irr_hbm, irr_ref), (place_hbm, place_ref),
        (par_hbm, par_ref),
    ]
    copies = [pltpu.make_async_copy(a, b, sems.at[n]) for n, (a, b) in enumerate(pairs)]
    for copy in copies:
        copy.start()
    share = rows // groups
    first = lax.axis_index("col") * mine
    other_first = lax.rem(lax.axis_index("col") + half, groups) * mine
    step = depth * LANES
    for m in range(mine):
        at = pl.ds(m * step, step)
        term_ref[at, :] = jnp.concatenate(halves(int_ref[at, :]), axis=1)
    for copy in copies:
        copy.wait()
    low, count = (usual, mine * depth - usual) if late else (0, usual)
    for m in range(mine):
        cols = []
        for k in range(depth):
            source = src_ref[m, k]
            place = place_ref[0, source]
            live = (k < cnt_ref[m]) & (irr_ref[source] == irr_ref[first + m])
            at = jnp.clip(place - low, 0, count - 1)
            block = jnp.concatenate(
                [
                    got_ref[pl.ds(r * count + at, groups, stride=share * count), :]
                    for r in range(share)
                ],
                axis=0,
            )
            if late:
                live = live & (place >= usual)
            else:
                live = live & (place < usual)
                owned = (source >= first) & (source < first + mine)
                own = jnp.where(owned, source - first, 0)
                own_block = extra_ref[:, pl.ds(pl.multiple_of(own * LANES, LANES), LANES)]
                block = jnp.where(owned, own_block, block)
            cols.append(jnp.where(live, block, 0.0))
        left_high, left_low = halves(jnp.concatenate(cols, axis=1))
        sums = jnp.dot(
            jnp.concatenate([left_high, left_low], axis=0),
            term_ref[pl.ds(m * step, step), :],
            preferred_element_type=jnp.float32,
        )
        sums = sums[:, :LANES] + sums[:, LANES:]
        sums = sums[:rows] + sums[rows:]
        if late:
            sums = sums + extra_ref[m]
        out_ref[m] = sums
        turned_ref[par_ref[first + m] - other_first] = sums


def finish(mine, rows, lad_ref, mir_ref, occ_ref, virt_ref, out_ref):
    row = lax.broadcasted_iota(jnp.int32, (rows, rows), 0)
    col = lax.broadcasted_iota(jnp.int32, (rows, rows), 1)
    occ = jnp.sum(jnp.where(row == col, occ_ref[...], 0.0), axis=1, keepdims=True)
    for m in range(mine):
        lanes = pl.ds(m * LANES, LANES)
        out_ref[:, lanes] = (lad_ref[m] + mir_ref[m]) / (occ - virt_ref[:, lanes])


def shards(amplitudes, integrals, sources, counts, tile_irrep, partner, occ_energy, virt_energy):
    rows = amplitudes.shape[0]
    mine, depth, width, _ = integrals.shape
    tiles = tile_irrep.shape[0]
    cols = lax.axis_size("col")
    heights = lax.axis_size("row")
    slots = mine * depth
    share = rows // cols
    chunk = share * mine + tiles // LANES
    f32 = jnp.float32

    i32 = jnp.int32
    usual = USUAL
    left = slots - usual

    def call(body, out, *args, specs, outs=None, scratch=(), flops=0, moved=0, room=16):
        return pl.pallas_call(
            body,
            out_shape=[jax.ShapeDtypeStruct(shape, dtype) for shape, dtype in out],
            in_specs=specs,
            out_specs=outs or [VMEM] * len(out),
            scratch_shapes=scratch,
            compiler_params=pltpu.CompilerParams(vmem_limit_bytes=room * 1024 * 1024),
            cost_estimate=pl.CostEstimate(flops=flops, bytes_accessed=moved, transcendentals=0),
        )(*args)

    sent, place = call(
        lambda *refs: spread(cols, mine, depth, rows, tiles, *refs),
        [((cols * chunk, LANES), f32), ((1, tiles), i32)],
        sources, counts, tile_irrep, tile_irrep.reshape(1, tiles), amplitudes,
        specs=[HBM] * 5,
        scratch=[
            pltpu.SMEM(sources.shape, i32),
            pltpu.SMEM(counts.shape, i32),
            pltpu.SMEM((tiles,), i32),
            pltpu.VMEM((1, tiles), i32),
            pltpu.VMEM(amplitudes.shape, f32),
            pltpu.SemaphoreType.DMA((5,)),
        ],
        moved=2 * amplitudes.size * 4,
        room=63,
    )
    got = lax.all_to_all(sent.reshape(cols, chunk, 1, LANES), "col", 0, 0)
    sent, rest, more = call(
        lambda *refs: pick(cols, mine, slots, usual, share, tiles, *refs),
        [
            ((cols * share * usual, LANES), f32),
            ((cols * share * left, LANES), f32),
            ((1,), i32),
        ],
        got.reshape(cols * chunk, LANES),
        specs=[VMEM],
        outs=[VMEM, VMEM, SMEM],
        scratch=[pltpu.VMEM((cols * slots, tiles), jnp.bfloat16)],
        flops=4 * cols * slots * tiles * share * LANES,
        moved=cols * slots * share * LANES * 4,
    )
    got = lax.all_to_all(sent.reshape(cols, share * usual, 1, LANES), "col", 0, 0)

    def products(late, extra, got):
        return call(
            lambda *refs: multiply(late, cols, cols // 2, mine, depth, rows, usual, *refs),
            [((mine, rows, width), f32)] * 2,
            partner, sources, counts, tile_irrep, place, extra, got.reshape(-1, LANES),
            integrals.reshape(mine * depth * width, width),
            specs=[HBM] * 5 + [VMEM] * 3,
            scratch=[
                pltpu.SMEM((tiles,), i32),
                pltpu.SMEM(sources.shape, i32),
                pltpu.SMEM(counts.shape, i32),
                pltpu.SMEM((tiles,), i32),
                pltpu.SMEM((1, tiles), i32),
                pltpu.VMEM((mine * depth * width, 2 * width), jnp.bfloat16),
                pltpu.SemaphoreType.DMA((5,)),
            ],
            flops=8 * rows * mine * depth * width * width,
            moved=integrals.size * 4 + got.size * 4,
        )

    pairs = [
        (r * cols + c, (r + heights // 2) % heights * cols + (c + cols // 2) % cols)
        for r in range(heights)
        for c in range(cols)
    ]

    def close(ladder, mirrored, rest):
        return call(
            lambda *refs: finish(mine, rows, *refs),
            [((rows, mine * width), f32)],
            ladder, mirrored, occ_energy.reshape(1, rows),
            virt_energy.reshape(1, mine * width),
            specs=[VMEM] * 4,
            moved=4 * rows * mine * width * 3,
        )[0]

    def amend(ladder, mirrored, rest):
        rest = lax.all_to_all(rest.reshape(cols, share * left, 1, LANES), "col", 0, 0)
        ladder, turned = products(True, ladder, rest)
        return close(ladder, lax.ppermute(turned, ("row", "col"), pairs), rest)

    ladder, turned = products(False, amplitudes, got)
    more, turned = lax.optimization_barrier((more, turned))
    mirrored = lax.ppermute(turned, ("row", "col"), pairs)
    return lax.cond(more[0] > 0, amend, close, ladder, mirrored, rest)


def solution(mesh):
    placed = (
        P("row", "col"),
        P("col", None, None, None),
        P("col", None),
        P("col"),
        P(),
        P(),
        P("row"),
        P("col"),
    )
    return jax.shard_map(
        shards, mesh=mesh, in_specs=placed, out_specs=P("row", "col"), check_vma=False
    )
```
